512 devices in a mesh: lat: 8 (over y, x_hi), lon: 64 (over z, x_lo, core).
Axes of the slice: x: 4 (x_hi: 2, x_lo: 2; x = x_hi * 2 + x_lo), y: 4, z: 16, core: 2. Of those that a mesh axis runs over, the one named last changes fastest.
Arguments:
- tokens: bfloat16 [96, 768, 512], P('lat', 'lon'), may hold values from -40 to 40
- cotangent: bfloat16 [96, 768, 512], P('lat', 'lon'), may hold values from -48 to 48
- w_query: bfloat16 [512, 512], replicated, may hold values from -0.25 to 0.25
- w_key: bfloat16 [512, 512], replicated, may hold values from -0.25 to 0.25
- w_value: bfloat16 [512, 512], replicated, may hold values from -0.25 to 0.25
- w_output: bfloat16 [512, 512], replicated, may hold values from -0.25 to 0.25
Outputs:
- d_tokens: bfloat16 [96, 768, 512], P('lat', 'lon')
- d_output: float32 [512, 512], replicated
The draws below stay inside these ranges and needn't reach their ends.
All inputs are finite; a program needn't handle non-finite values.
Results may differ from the reference program's by a relative error of at most 0.01.
The reference program's roundings to bfloat16 on the way count: a program that leaves them out, or rounds other values in their place, can miss the bound.
Values may be sent and summed in bfloat16 or wider, within the bound.
No kernel may reach another device: no remote copies, remote signals or barrier semaphores. Data moves between devices by JAX's collectives and lax.ppermute only.
A program may use at most 64 MiB of HBM per device.

```python
import math
import jax
import jax.numpy as jnp
from jax import lax

D = 512
HEADS = 16
WIN = 12
TL = 12
TC = 12
SHIFT = 6
NLAT = 96
NLON = 768


def draw_tokens(key, part):
    key = jax.random.fold_in(key, 11)
    base_key = jax.random.fold_in(key, 0)
    base = jax.random.normal(base_key, (NLAT, NLON, D), jnp.float32)
    return jnp.clip(base, -4.0, 4.0).astype(jnp.bfloat16)


def draw_cotangent(key, part):
    key = jax.random.fold_in(key, 23)
    base_key, offset_key = jax.random.split(key, 2)
    base = jnp.clip(jax.random.normal(base_key, (NLAT, NLON, D), jnp.float32), -6.0, 6.0)
    offset = jax.random.randint(offset_key, (), 0, D)
    row_band = jnp.arange(NLAT, dtype=jnp.int32) // TL
    col_band = jnp.arange(NLON, dtype=jnp.int32) // TC
    device = row_band[:, None] * (NLON // TC) + col_band[None, :]
    paired = (device + offset) % D
    feature = jnp.arange(D, dtype=jnp.int32)
    boost = jnp.where(paired[:, :, None] == feature[None, None, :], 8.0, 1.0)
    return (base * boost).astype(jnp.bfloat16)


def centred(stream_key, shape, width, limit, kind=jnp.bfloat16):
    return jnp.clip(width * jax.random.normal(stream_key, shape, jnp.float32), -limit, limit).astype(kind)


def setup_inputs(seed: int = 0) -> dict:
    arg_keys = jax.random.split(jax.random.key(seed), 7)
    return {
        "tokens": draw_tokens(jax.random.fold_in(arg_keys[6], 71), 0),
        "cotangent": draw_cotangent(jax.random.fold_in(arg_keys[6], 71), 0),
        "w_query": centred(arg_keys[2], (D, D), D ** -0.5, 0.25),
        "w_key": centred(arg_keys[3], (D, D), D ** -0.5, 0.25),
        "w_value": centred(arg_keys[4], (D, D), D ** -0.5, 0.25),
        "w_output": centred(arg_keys[5], (D, D), D ** -0.5, 0.25),
    }


def to_windows(field, window):
    n_rows, n_cols, depth = field.shape
    blocks = field.reshape(n_rows // window, window, n_cols // window, window, depth)
    return blocks.transpose(0, 2, 1, 3, 4).reshape(-1, window * window, depth)

def from_windows(packed, window, n_rows, n_cols):
    depth = packed.shape[-1]
    blocks = packed.reshape(n_rows // window, n_cols // window, window, window, depth)
    return blocks.transpose(0, 2, 1, 3, 4).reshape(n_rows, n_cols, depth)

def window_backward(windows, cot_windows, labels, w_query, w_key, w_value, w_output, n_heads):
    n_win, n_pts, model_width = windows.shape
    head_dim = model_width // n_heads
    factor_qk = 1.0 / math.sqrt(head_dim)
    flat_tokens = windows.reshape(n_win * n_pts, model_width)
    w_joint = jnp.concatenate([w_query, w_key, w_value], axis=1)
    projected = jnp.dot(flat_tokens, w_joint, preferred_element_type=jnp.float32).astype(jnp.bfloat16)
    shaped = projected.reshape(n_win, n_pts, 3, n_heads, head_dim)
    queries = shaped[:, :, 0].astype(jnp.float32)
    key_rows = shaped[:, :, 1].astype(jnp.float32)
    value_rows = shaped[:, :, 2].astype(jnp.float32)
    logits = factor_qk * jnp.einsum('wqhd,wkhd->whqk', queries, key_rows)
    allowed = (labels[:, :, None] == labels[:, None, :])[:, None]
    logits = jnp.where(allowed, logits, -1e+30)
    peak = lax.optimization_barrier(jnp.max(logits, axis=-1, keepdims=True))
    raised = jnp.exp(logits - peak)
    probs = raised / lax.optimization_barrier(jnp.sum(raised, axis=-1, keepdims=True))
    probs_low = probs.astype(jnp.bfloat16).astype(jnp.float32)
    attended = jnp.einsum('whqk,wkhd->wqhd', probs_low, value_rows).astype(jnp.bfloat16)
    attended_flat = attended.reshape(n_win * n_pts, model_width)
    upstream = cot_windows.reshape(n_win * n_pts, model_width)
    output_term = jnp.dot(attended_flat.T, upstream, preferred_element_type=jnp.float32)
    d_attended = jnp.dot(upstream, w_output.T, preferred_element_type=jnp.float32).astype(jnp.bfloat16)
    d_attended = d_attended.reshape(n_win, n_pts, n_heads, head_dim).astype(jnp.float32)
    d_probs = jnp.einsum('wqhd,wkhd->whqk', d_attended, value_rows)
    d_values = jnp.einsum('whqk,wqhd->wkhd', probs_low, d_attended).astype(jnp.bfloat16)
    row_inner = lax.optimization_barrier(jnp.sum(probs * d_probs, axis=-1, keepdims=True))
    d_logits = (factor_qk * probs * (d_probs - row_inner)).astype(jnp.bfloat16).astype(jnp.float32)
    d_queries = jnp.einsum('whqk,wkhd->wqhd', d_logits, key_rows).astype(jnp.bfloat16)
    d_keys = jnp.einsum('whqk,wqhd->wkhd', d_logits, queries).astype(jnp.bfloat16)
    joined = jnp.stack([d_queries, d_keys, d_values], axis=2).reshape(n_win * n_pts, 3 * model_width)
    d_flat = jnp.dot(joined, w_joint.T, preferred_element_type=jnp.float32)
    return (d_flat.reshape(n_win, n_pts, model_width), output_term)

def reference(tokens, cotangent, w_query, w_key, w_value, w_output):
    rolled = jnp.roll(tokens, (-SHIFT, -SHIFT), (0, 1))
    rolled_cot = jnp.roll(cotangent, (-SHIFT, -SHIFT), (0, 1))
    region = (jnp.arange(NLAT) >= NLAT - SHIFT).astype(jnp.int32)
    strips = rolled.reshape(NLAT // WIN, WIN, NLON, D)
    cot_strips = rolled_cot.reshape(NLAT // WIN, WIN, NLON, D)
    region_strips = region.reshape(NLAT // WIN, WIN)

    def one_strip(packed):
        strip, cot_strip, labels_row = packed
        labels_tile = jnp.broadcast_to(labels_row[:, None, None], (WIN, NLON, 1))
        labels = to_windows(labels_tile, WIN)[:, :, 0]
        d_win, output_term = window_backward(to_windows(strip, WIN), to_windows(cot_strip, WIN), labels, w_query, w_key, w_value, w_output, HEADS)
        d_strip = from_windows(d_win.astype(jnp.bfloat16), WIN, WIN, NLON)
        return (d_strip, output_term)
    d_strips, output_terms = lax.map(one_strip, (strips, cot_strips, region_strips))
    d_rolled = d_strips.reshape(NLAT, NLON, D)
    d_tokens = jnp.roll(d_rolled, (SHIFT, SHIFT), (0, 1))
    summed = lax.optimization_barrier(jnp.sum(output_terms, axis=0))
    sum_squares = jnp.sum(summed * summed)
    clip_factor = jnp.minimum(jnp.float32(1.0), jnp.float32(D) / (jnp.sqrt(sum_squares) + 1e-06))
    return (d_tokens, summed * clip_factor)
```

```python
import math

import jax
import jax.numpy as jnp
from jax import lax
from jax.experimental import pallas as pl
from jax.experimental.pallas import tpu as pltpu
from jax.sharding import Mesh
from jax.sharding import PartitionSpec as P

HEADS = 16
DH = 32
D = 512
HALF = 6
QUAD = HALF * HALF
N = 4 * QUAD
SPLIT = ("y", "xh", "z", "xl", "core")
LAT = ("y", "xh")
LON = ("z", "xl", "core")
PLANE = ("y", "xh", "xl", "core")
F32 = jnp.float32
BF16 = jnp.bfloat16
NT = (((1,), (1,)), ((), ()))
VMEM = pl.BlockSpec(memory_space=pltpu.VMEM)
SMEM = pl.BlockSpec(memory_space=pltpu.SMEM)
PARAMS = pltpu.CompilerParams(vmem_limit_bytes=40 * 1024 * 1024)


def dot(a, b, dims=(((1,), (0,)), ((), ()))):
    return lax.dot_general(a, b, dims, preferred_element_type=F32)


def window_kernel(
    last_ref, tok_ref, cot_ref, lon_ref, lat_ref, diag_ref, wq_ref, wk_ref, wv_ref, wo_ref,
    g_ref, own_out, lon_out, lat_out, diag_out,
    x_s, c_s, ot_s, dqt_s, dkt_s, dvt_s, dr_s,
):
    for i in range(HALF):
        x_s[HALF * i : HALF * (i + 1), :] = tok_ref[HALF + i].astype(F32)[HALF:]
        c_s[HALF * i : HALF * (i + 1), :] = cot_ref[HALF + i].astype(F32)[HALF:]
        for part, ref in ((1, lon_ref), (2, lat_ref), (3, diag_ref)):
            at = QUAD * part + HALF * i
            x_s[at : at + HALF, :] = ref[0, i].astype(F32)
            c_s[at : at + HALF, :] = ref[1, i].astype(F32)
    x = x_s[...].astype(BF16)
    c = c_s[...].astype(BF16)
    q = dot(x, wq_ref[...]).astype(BF16)
    k = dot(x, wk_ref[...]).astype(BF16)
    v = dot(x, wv_ref[...]).astype(BF16)
    dot_t = dot(wo_ref[...], c, NT).astype(BF16)
    qt = q.T
    kt = k.T
    vt = v.T
    factor = 1.0 / math.sqrt(DH)
    row = lax.broadcasted_iota(jnp.int32, (N, N), 0) >= 2 * QUAD
    col = lax.broadcasted_iota(jnp.int32, (N, N), 1) >= 2 * QUAD
    bias = jnp.where(jnp.logical_and(row != col, last_ref[0] == 1), F32(-1e30), F32(0.0))
    for h in range(HEADS):
        at = slice(DH * h, DH * (h + 1))
        kh, vh = k[:, at], v[:, at]
        qth, kth, vth, doth = qt[at], kt[at], vt[at], dot_t[at]
        s = dot(kh, qth) * factor + bias
        e = jnp.exp(s - jnp.max(s, axis=0, keepdims=True))
        p = e * (1.0 / jnp.sum(e, axis=0, keepdims=True))
        pb = p.astype(BF16)
        ot_s[at, :] = dot(vth, pb).astype(BF16)
        dp = dot(vh, doth)
        dvt_s[at, :] = dot(doth, pb, NT).astype(BF16)
        inner = jnp.sum(p * dp, axis=0, keepdims=True)
        ds = (factor * p * (dp - inner)).astype(BF16)
        dqt_s[at, :] = dot(kth, ds).astype(BF16)
        dkt_s[at, :] = dot(qth, ds, NT).astype(BF16)
    g_ref[...] = dot(ot_s[...], c).astype(BF16)
    dr_s[...] = (
        dot(dqt_s[...].T, wq_ref[...], NT)
        + dot(dkt_s[...].T, wk_ref[...], NT)
        + dot(dvt_s[...].T, wv_ref[...], NT)
    )
    for part, ref in enumerate((own_out, lon_out, lat_out, diag_out)):
        for i in range(HALF):
            at = QUAD * part + HALF * i
            ref[i] = dr_s[at : at + HALF, :].astype(BF16)


def window_call(last, tokens, cotangent, lon, lat, diag, wq, wk, wv, wo):
    quad = jax.ShapeDtypeStruct((HALF, HALF, D), BF16)
    return pl.pallas_call(
        window_kernel,
        out_shape=(jax.ShapeDtypeStruct((D, D), BF16), quad, quad, quad, quad),
        in_specs=[SMEM] + [VMEM] * 9,
        out_specs=(VMEM,) * 5,
        scratch_shapes=[
            pltpu.VMEM((N, D), F32),
            pltpu.VMEM((N, D), F32),
            pltpu.VMEM((D, N), BF16),
            pltpu.VMEM((D, N), BF16),
            pltpu.VMEM((D, N), BF16),
            pltpu.VMEM((D, N), BF16),
            pltpu.VMEM((N, D), F32),
        ],
        compiler_params=PARAMS,
    )(last, tokens, cotangent, lon, lat, diag, wq, wk, wv, wo)


def sum_kernel(in_ref, out_ref):
    total = in_ref[0].astype(F32)
    for i in range(1, in_ref.shape[0]):
        total = total + in_ref[i].astype(F32)
    total = total.astype(BF16)
    for i in range(out_ref.shape[0]):
        out_ref[i] = total


def sum_and_repeat(parts, copies):
    return pl.pallas_call(
        sum_kernel,
        out_shape=jax.ShapeDtypeStruct((copies,) + parts.shape[1:], BF16),
        in_specs=[VMEM],
        out_specs=VMEM,
        compiler_params=PARAMS,
    )(parts)


def finish_kernel(g_ref, own_ref, lon_ref, lat_ref, diag_ref, dtok_ref, dout_ref):
    g = g_ref[...].astype(F32)
    norm = jnp.sqrt(jnp.sum(g * g, keepdims=True))
    dout_ref[...] = g * jnp.minimum(F32(1.0), F32(D) / (norm + 1e-6))
    for i in range(HALF):
        top = (diag_ref[i].astype(F32), lat_ref[i].astype(F32))
        dtok_ref[i] = jnp.concatenate(top, axis=0).astype(BF16)
        bottom = (lon_ref[i].astype(F32), own_ref[i].astype(F32))
        dtok_ref[HALF + i] = jnp.concatenate(bottom, axis=0).astype(BF16)


def finish_call(g, own, lon, lat, diag):
    return pl.pallas_call(
        finish_kernel,
        out_shape=(
            jax.ShapeDtypeStruct((2 * HALF, 2 * HALF, D), BF16),
            jax.ShapeDtypeStruct((D, D), F32),
        ),
        in_specs=[VMEM] * 5,
        out_specs=(VMEM, VMEM),
        compiler_params=PARAMS,
    )(g, own, lon, lat, diag)


def shifted(value, lat_step, lon_step):
    axes = (LAT if lat_step else ()) + (LON if lon_step else ())
    n_lat = lax.axis_size(LAT) if lat_step else 1
    n_lon = lax.axis_size(LON) if lon_step else 1
    pairs = []
    for a in range(n_lat):
        for b in range(n_lon):
            to = (a + lat_step) % n_lat * n_lon + (b + lon_step) % n_lon
            pairs.append((a * n_lon + b, to))
    return lax.ppermute(value, axes, pairs)


def per_device(tokens, cotangent, w_query, w_key, w_value, w_output):
    lat = shifted(jnp.stack([tokens[:HALF, HALF:], cotangent[:HALF, HALF:]]), -1, 0)
    lon = shifted(jnp.stack([tokens[HALF:, :HALF], cotangent[HALF:, :HALF]]), 0, -1)
    diag = shifted(jnp.stack([tokens[:HALF, :HALF], cotangent[:HALF, :HALF]]), -1, -1)
    last = (lax.axis_index(LAT) == lax.axis_size(LAT) - 1).astype(jnp.int32).reshape(1)
    g, own, lon, lat, diag = window_call(
        last, tokens, cotangent, lon, lat, diag, w_query, w_key, w_value, w_output
    )
    lat = shifted(lat, 1, 0)
    lon = shifted(lon, 0, 1)
    diag = shifted(diag, 1, 1)
    n_plane = lax.axis_size(PLANE)
    n_z = lax.axis_size("z")
    parts = g.reshape(n_plane, D // n_plane, D)
    parts = lax.all_to_all(parts, PLANE, 0, 0, tiled=True)
    parts = lax.all_to_all(sum_and_repeat(parts, n_z), "z", 0, 0, tiled=True)
    parts = lax.all_to_all(sum_and_repeat(parts, n_plane), PLANE, 0, 0, tiled=True)
    return finish_call(parts.reshape(D, D), own, lon, lat, diag)


def solution(mesh):
    fine = Mesh(mesh.devices.reshape(4, 2, 16, 2, 2), SPLIT)
    tiles = P(LAT, LON, None)
    return jax.shard_map(
        per_device,
        mesh=fine,
        in_specs=(tiles, tiles, P(), P(), P(), P()),
        out_specs=(tiles, P()),
        check_vma=False,
    )
```

```python
import math

import jax
import jax.numpy as jnp
from jax import lax
from jax.experimental import pallas as pl
from jax.experimental.pallas import tpu as pltpu
from jax.sharding import Mesh
from jax.sharding import PartitionSpec as P

HEADS = 16
DH = 32
D = 512
HALF = 6
FACTOR = 1.0 / math.sqrt(DH)
QUAD = HALF * HALF
N = 4 * QUAD
SPLIT = ("y", "xh", "z", "xl", "core")
LAT = ("y", "xh")
LON = ("z", "xl", "core")
PLANE = ("y", "xh", "xl", "core")
F32 = jnp.float32
BF16 = jnp.bfloat16
NT = (((1,), (1,)), ((), ()))
VMEM = pl.BlockSpec(memory_space=pltpu.VMEM)
ANY = pl.BlockSpec(memory_space=pl.ANY)
HBM = pl.BlockSpec(memory_space=pltpu.HBM)
SMEM = pl.BlockSpec(memory_space=pltpu.SMEM)
MIB = 1024 * 1024
PARAMS = pltpu.CompilerParams(vmem_limit_bytes=12 * MIB)
WIDE = pltpu.CompilerParams(vmem_limit_bytes=52 * MIB)


def dot(a, b, dims=(((1,), (0,)), ((), ()))):
    return lax.dot_general(a, b, dims, preferred_element_type=F32)


def load_kernel(wq_ref, wk_ref, wv_ref, wo_ref, q_out, k_out, v_out, o_out, sems):
    pairs = ((wq_ref, q_out), (wk_ref, k_out), (wv_ref, v_out), (wo_ref, o_out))
    copies = [
        pltpu.make_async_copy(source, target, sems.at[i])
        for i, (source, target) in enumerate(pairs)
    ]
    for copy in copies:
        copy.start()
    for copy in copies:
        copy.wait()


def load_weights(*weights):
    return pl.pallas_call(
        load_kernel,
        out_shape=tuple(jax.ShapeDtypeStruct(w.shape, w.dtype) for w in weights),
        in_specs=[HBM] * 4,
        out_specs=(VMEM,) * 4,
        scratch_shapes=[pltpu.SemaphoreType.DMA((4,))],
        compiler_params=WIDE,
    )(*weights)


def score_bias(last):
    row = lax.broadcasted_iota(jnp.int32, (N, N), 0) >= 2 * QUAD
    col = lax.broadcasted_iota(jnp.int32, (N, N), 1) >= 2 * QUAD
    return jnp.where(jnp.logical_and(row != col, last == 1), F32(-1e30), F32(0.0))


def softmax_t(kh, qth, bias):
    s = dot(kh, qth) * FACTOR + bias
    e = jnp.exp(s - jnp.max(s, axis=0, keepdims=True))
    return e * (1.0 / jnp.sum(e, axis=0, keepdims=True))


def forward_kernel(
    last_ref, tok_ref, cot_ref, lon_ref, lat_ref, diag_ref, wq_ref, wk_ref, wv_ref,
    g_ref, q_ref, k_ref, v_ref, c_ref,
    x_s, c_s, ot_s,
):
    for i in range(HALF):
        x_s[HALF * i : HALF * (i + 1), :] = tok_ref[HALF + i].astype(F32)[HALF:]
        c_s[HALF * i : HALF * (i + 1), :] = cot_ref[HALF + i].astype(F32)[HALF:]
        for part, ref in ((1, lon_ref), (2, lat_ref), (3, diag_ref)):
            at = QUAD * part + HALF * i
            x_s[at : at + HALF, :] = ref[0, i].astype(F32)
            c_s[at : at + HALF, :] = ref[1, i].astype(F32)
    x = x_s[...].astype(BF16)
    c = c_s[...].astype(BF16)
    q = dot(x, wq_ref[...]).astype(BF16)
    k = dot(x, wk_ref[...]).astype(BF16)
    v = dot(x, wv_ref[...]).astype(BF16)
    qt = q.T
    vt = v.T
    bias = score_bias(last_ref[0])
    for h in range(HEADS):
        at = slice(DH * h, DH * (h + 1))
        pb = softmax_t(k[:, at], qt[at], bias).astype(BF16)
        ot_s[at, :] = dot(vt[at], pb).astype(BF16)
    g_ref[...] = dot(ot_s[...], c).astype(BF16)
    q_ref[...] = q
    k_ref[...] = k
    v_ref[...] = v
    c_ref[...] = c


def forward_call(last, tokens, cotangent, lon, lat, diag, wq, wk, wv):
    flat = jax.ShapeDtypeStruct((N, D), BF16)
    return pl.pallas_call(
        forward_kernel,
        out_shape=(jax.ShapeDtypeStruct((D, D), BF16), flat, flat, flat, flat),
        in_specs=[SMEM] + [VMEM] * 8,
        out_specs=(VMEM,) * 5,
        scratch_shapes=[
            pltpu.VMEM((N, D), F32),
            pltpu.VMEM((N, D), F32),
            pltpu.VMEM((D, N), BF16),
        ],
        compiler_params=PARAMS,
    )(last, tokens, cotangent, lon, lat, diag, wq, wk, wv)


def backward_kernel(
    last_ref, q_ref, k_ref, v_ref, c_ref, wq_ref, wk_ref, wv_ref, wo_ref,
    own_out, lon_out, lat_out, diag_out,
    dqt_s, dkt_s, dvt_s, dr_s,
):
    k = k_ref[...]
    v = v_ref[...]
    qt = q_ref[...].T
    kt = k.T
    dot_t = dot(wo_ref[...], c_ref[...], NT).astype(BF16)
    bias = score_bias(last_ref[0])
    for h in range(HEADS):
        at = slice(DH * h, DH * (h + 1))
        p = softmax_t(k[:, at], qt[at], bias)
        dp = dot(v[:, at], dot_t[at])
        dvt_s[at, :] = dot(dot_t[at], p.astype(BF16), NT).astype(BF16)
        inner = jnp.sum(p * dp, axis=0, keepdims=True)
        ds = (FACTOR * p * (dp - inner)).astype(BF16)
        dqt_s[at, :] = dot(kt[at], ds).astype(BF16)
        dkt_s[at, :] = dot(qt[at], ds, NT).astype(BF16)
    dr_s[...] = (
        dot(dqt_s[...].T, wq_ref[...], NT)
        + dot(dkt_s[...].T, wk_ref[...], NT)
        + dot(dvt_s[...].T, wv_ref[...], NT)
    )
    for part, ref in enumerate((own_out, lon_out, lat_out, diag_out)):
        for i in range(HALF):
            at = QUAD * part + HALF * i
            ref[i] = dr_s[at : at + HALF, :].astype(BF16)


def backward_call(last, q, k, v, c, wq, wk, wv, wo):
    quad = jax.ShapeDtypeStruct((HALF, HALF, D), BF16)
    return pl.pallas_call(
        backward_kernel,
        out_shape=(quad, quad, quad, quad),
        in_specs=[SMEM] + [VMEM] * 8,
        out_specs=(VMEM,) * 4,
        scratch_shapes=[
            pltpu.VMEM((D, N), BF16),
            pltpu.VMEM((D, N), BF16),
            pltpu.VMEM((D, N), BF16),
            pltpu.VMEM((N, D), F32),
        ],
        compiler_params=PARAMS,
    )(last, q, k, v, c, wq, wk, wv, wo)


def sum_kernel(in_ref, *rest):
    out_ref = rest[-1]
    total = in_ref[0].astype(F32)
    for i in range(1, in_ref.shape[0]):
        total = total + in_ref[i].astype(F32)
    total = total.astype(BF16)
    for i in range(out_ref.shape[0]):
        out_ref[i] = total


def sum_and_repeat(parts, copies, *after):
    return pl.pallas_call(
        sum_kernel,
        out_shape=jax.ShapeDtypeStruct((copies,) + parts.shape[1:], BF16),
        in_specs=[VMEM] + [ANY] * len(after),
        out_specs=VMEM,
        compiler_params=PARAMS,
    )(parts, *after)


def finish_kernel(g_ref, own_ref, lon_ref, lat_ref, diag_ref, dtok_ref, dout_ref):
    g = g_ref[...].astype(F32)
    norm = jnp.sqrt(jnp.sum(g * g, keepdims=True))
    dout_ref[...] = g * jnp.minimum(F32(1.0), F32(D) / (norm + 1e-6))
    for i in range(HALF):
        top = (diag_ref[i].astype(F32), lat_ref[i].astype(F32))
        dtok_ref[i] = jnp.concatenate(top, axis=0).astype(BF16)
        bottom = (lon_ref[i].astype(F32), own_ref[i].astype(F32))
        dtok_ref[HALF + i] = jnp.concatenate(bottom, axis=0).astype(BF16)


def finish_call(g, own, lon, lat, diag):
    return pl.pallas_call(
        finish_kernel,
        out_shape=(
            jax.ShapeDtypeStruct((2 * HALF, 2 * HALF, D), BF16),
            jax.ShapeDtypeStruct((D, D), F32),
        ),
        in_specs=[VMEM] * 5,
        out_specs=(VMEM, VMEM),
        compiler_params=PARAMS,
    )(g, own, lon, lat, diag)


def shifted(value, lat_step, lon_step):
    axes = (LAT if lat_step else ()) + (LON if lon_step else ())
    n_lat = lax.axis_size(LAT) if lat_step else 1
    n_lon = lax.axis_size(LON) if lon_step else 1
    pairs = []
    for a in range(n_lat):
        for b in range(n_lon):
            to = (a + lat_step) % n_lat * n_lon + (b + lon_step) % n_lon
            pairs.append((a * n_lon + b, to))
    return lax.ppermute(value, axes, pairs)


def per_device(tokens, cotangent, w_query, w_key, w_value, w_output):
    lat = shifted(jnp.stack([tokens[:HALF, HALF:], cotangent[:HALF, HALF:]]), -1, 0)
    lon = shifted(jnp.stack([tokens[HALF:, :HALF], cotangent[HALF:, :HALF]]), 0, -1)
    diag = shifted(jnp.stack([tokens[:HALF, :HALF], cotangent[:HALF, :HALF]]), -1, -1)
    last = (lax.axis_index(LAT) == lax.axis_size(LAT) - 1).astype(jnp.int32).reshape(1)
    wq, wk, wv, wo = load_weights(w_query, w_key, w_value, w_output)
    g, q, k, v, c = forward_call(last, tokens, cotangent, lon, lat, diag, wq, wk, wv)
    n_plane = lax.axis_size(PLANE)
    n_z = lax.axis_size("z")
    parts = g.reshape(n_plane, D // n_plane, D)
    parts = lax.all_to_all(parts, PLANE, 0, 0, tiled=True)
    own, lon, lat, diag = backward_call(last, q, k, v, c, wq, wk, wv, wo)
    parts = lax.all_to_all(sum_and_repeat(parts, n_z, own), "z", 0, 0, tiled=True)
    lat = shifted(lat, 1, 0)
    lon = shifted(lon, 0, 1)
    diag = shifted(diag, 1, 1)
    parts = sum_and_repeat(parts, n_plane, lon, lat, diag)
    parts = lax.all_to_all(parts, PLANE, 0, 0, tiled=True)
    return finish_call(parts.reshape(D, D), own, lon, lat, diag)


def solution(mesh):
    fine = Mesh(mesh.devices.reshape(4, 2, 16, 2, 2), SPLIT)
    tiles = P(LAT, LON, None)
    return jax.shard_map(
        per_device,
        mesh=fine,
        in_specs=(tiles, tiles, P(), P(), P(), P()),
        out_specs=(tiles, P()),
        check_vma=False,
    )
```

```python
import math

import jax
import jax.numpy as jnp
from jax import lax
from jax.experimental import pallas as pl
from jax.experimental.pallas import tpu as pltpu
from jax.sharding import Mesh
from jax.sharding import PartitionSpec as P

HEADS = 16
DH = 32
D = 512
HALF = 6
FACTOR = 1.0 / math.sqrt(DH)
QUAD = HALF * HALF
N = 4 * QUAD
SPLIT = ("y", "xh", "z", "xl", "core")
LAT = ("y", "xh")
LON = ("z", "xl", "core")
PLANE = ("y", "xh", "xl", "core")
F32 = jnp.float32
BF16 = jnp.bfloat16
NT = (((1,), (1,)), ((), ()))
VMEM = pl.BlockSpec(memory_space=pltpu.VMEM)
ANY = pl.BlockSpec(memory_space=pl.ANY)
HBM = pl.BlockSpec(memory_space=pltpu.HBM)
SMEM = pl.BlockSpec(memory_space=pltpu.SMEM)
MIB = 1024 * 1024
PARAMS = pltpu.CompilerParams(vmem_limit_bytes=12 * MIB)
WIDE = pltpu.CompilerParams(vmem_limit_bytes=52 * MIB)


def dot(a, b, dims=(((1,), (0,)), ((), ()))):
    return lax.dot_general(a, b, dims, preferred_element_type=F32)


def load_kernel(wq_ref, wk_ref, wv_ref, wo_ref, q_out, k_out, v_out, o_out, sems):
    pairs = ((wq_ref, q_out), (wk_ref, k_out), (wv_ref, v_out), (wo_ref, o_out))
    copies = [
        pltpu.make_async_copy(source, target, sems.at[i])
        for i, (source, target) in enumerate(pairs)
    ]
    for copy in copies:
        copy.start()
    for copy in copies:
        copy.wait()


def load_weights(*weights):
    return pl.pallas_call(
        load_kernel,
        out_shape=tuple(jax.ShapeDtypeStruct(w.shape, w.dtype) for w in weights),
        in_specs=[HBM] * 4,
        out_specs=(VMEM,) * 4,
        scratch_shapes=[pltpu.SemaphoreType.DMA((4,))],
        compiler_params=WIDE,
    )(*weights)


def score_bias(last):
    row = lax.broadcasted_iota(jnp.int32, (N, N), 0) >= 2 * QUAD
    col = lax.broadcasted_iota(jnp.int32, (N, N), 1) >= 2 * QUAD
    return jnp.where(jnp.logical_and(row != col, last == 1), F32(-1e30), F32(0.0))


def softmax_t(scores, bias):
    s = scores * (FACTOR * math.log2(math.e)) + bias
    e = jnp.exp2(s - jnp.max(s, axis=0, keepdims=True))
    return e * (1.0 / jnp.sum(e, axis=0, keepdims=True))


def staggered(depth, before, between, after):
    rows = [slice(DH * h, DH * (h + 1)) for h in range(HEADS)]
    ready = {h: before(rows[h]) for h in range(depth)}
    done = {}
    for h in range(HEADS + depth):
        if h + depth < HEADS:
            ready[h + depth] = before(rows[h + depth])
        if h >= depth:
            after(rows[h - depth], done.pop(h - depth))
        if h < HEADS:
            done[h] = between(ready.pop(h))


def forward_kernel(
    last_ref, tok_ref, cot_ref, lon_ref, lat_ref, diag_ref, wq_ref, wk_ref, wv_ref,
    g_ref, q_ref, k_ref, v_ref, c_ref,
    x_s, c_s, ot_s,
):
    for i in range(HALF):
        x_s[HALF * i : HALF * (i + 1), :] = tok_ref[HALF + i].astype(F32)[HALF:]
        c_s[HALF * i : HALF * (i + 1), :] = cot_ref[HALF + i].astype(F32)[HALF:]
        for part, ref in ((1, lon_ref), (2, lat_ref), (3, diag_ref)):
            at = QUAD * part + HALF * i
            x_s[at : at + HALF, :] = ref[0, i].astype(F32)
            c_s[at : at + HALF, :] = ref[1, i].astype(F32)
    x = x_s[...].astype(BF16)
    c = c_s[...].astype(BF16)
    q = dot(x, wq_ref[...]).astype(BF16)
    k = dot(x, wk_ref[...]).astype(BF16)
    v = dot(x, wv_ref[...]).astype(BF16)
    qt = q.T
    vt = v.T
    bias = score_bias(last_ref[0])

    def before(at):
        return dot(k[:, at], qt[at])

    def between(scores):
        return softmax_t(scores, bias).astype(BF16)

    def after(at, pb):
        ot_s[at, :] = dot(vt[at], pb).astype(BF16)

    staggered(3, before, between, after)
    g_ref[...] = dot(ot_s[...], c).astype(BF16)
    q_ref[...] = q
    k_ref[...] = k
    v_ref[...] = v
    c_ref[...] = c


def forward_call(last, tokens, cotangent, lon, lat, diag, wq, wk, wv):
    flat = jax.ShapeDtypeStruct((N, D), BF16)
    return pl.pallas_call(
        forward_kernel,
        out_shape=(jax.ShapeDtypeStruct((D, D), BF16), flat, flat, flat, flat),
        in_specs=[SMEM] + [VMEM] * 8,
        out_specs=(VMEM,) * 5,
        scratch_shapes=[
            pltpu.VMEM((N, D), F32),
            pltpu.VMEM((N, D), F32),
            pltpu.VMEM((D, N), BF16),
        ],
        compiler_params=PARAMS,
    )(last, tokens, cotangent, lon, lat, diag, wq, wk, wv)


def backward_kernel(
    last_ref, q_ref, k_ref, v_ref, c_ref, wq_ref, wk_ref, wv_ref, wo_ref,
    own_out, lon_out, lat_out, diag_out,
    dqt_s, dkt_s, dvt_s, dr_s,
):
    k = k_ref[...]
    v = v_ref[...]
    qt = q_ref[...].T
    kt = k.T
    dot_t = dot(wo_ref[...], c_ref[...], NT).astype(BF16)
    bias = score_bias(last_ref[0])

    def before(at):
        return dot(k[:, at], qt[at]), dot(v[:, at], dot_t[at])

    def between(products):
        scores, dp = products
        p = softmax_t(scores, bias)
        inner = jnp.sum(p * dp, axis=0, keepdims=True)
        return p.astype(BF16), (FACTOR * p * (dp - inner)).astype(BF16)

    def after(at, factors):
        pb, ds = factors
        dvt_s[at, :] = dot(dot_t[at], pb, NT).astype(BF16)
        dqt_s[at, :] = dot(kt[at], ds).astype(BF16)
        dkt_s[at, :] = dot(qt[at], ds, NT).astype(BF16)

    staggered(2, before, between, after)
    dr_s[...] = (
        dot(dqt_s[...].T, wq_ref[...], NT)
        + dot(dkt_s[...].T, wk_ref[...], NT)
        + dot(dvt_s[...].T, wv_ref[...], NT)
    )
    for part, ref in enumerate((own_out, lon_out, lat_out, diag_out)):
        for i in range(HALF):
            at = QUAD * part + HALF * i
            ref[i] = dr_s[at : at + HALF, :].astype(BF16)


def backward_call(last, q, k, v, c, wq, wk, wv, wo):
    quad = jax.ShapeDtypeStruct((HALF, HALF, D), BF16)
    return pl.pallas_call(
        backward_kernel,
        out_shape=(quad, quad, quad, quad),
        in_specs=[SMEM] + [VMEM] * 8,
        out_specs=(VMEM,) * 4,
        scratch_shapes=[
            pltpu.VMEM((D, N), BF16),
            pltpu.VMEM((D, N), BF16),
            pltpu.VMEM((D, N), BF16),
            pltpu.VMEM((N, D), F32),
        ],
        compiler_params=PARAMS,
    )(last, q, k, v, c, wq, wk, wv, wo)


def sum_kernel(in_ref, *rest):
    out_ref = rest[-1]
    total = in_ref[0].astype(F32)
    for i in range(1, in_ref.shape[0]):
        total = total + in_ref[i].astype(F32)
    total = total.astype(BF16)
    for i in range(out_ref.shape[0]):
        out_ref[i] = total


def sum_and_repeat(parts, copies, *after):
    return pl.pallas_call(
        sum_kernel,
        out_shape=jax.ShapeDtypeStruct((copies,) + parts.shape[1:], BF16),
        in_specs=[VMEM] + [ANY] * len(after),
        out_specs=VMEM,
        compiler_params=PARAMS,
    )(parts, *after)


def finish_kernel(g_ref, own_ref, lon_ref, lat_ref, diag_ref, dtok_ref, dout_ref):
    g = g_ref[...].astype(F32)
    norm = jnp.sqrt(jnp.sum(g * g, keepdims=True))
    dout_ref[...] = g * jnp.minimum(F32(1.0), F32(D) / (norm + 1e-6))
    for i in range(HALF):
        top = (diag_ref[i].astype(F32), lat_ref[i].astype(F32))
        dtok_ref[i] = jnp.concatenate(top, axis=0).astype(BF16)
        bottom = (lon_ref[i].astype(F32), own_ref[i].astype(F32))
        dtok_ref[HALF + i] = jnp.concatenate(bottom, axis=0).astype(BF16)


def finish_call(g, own, lon, lat, diag):
    return pl.pallas_call(
        finish_kernel,
        out_shape=(
            jax.ShapeDtypeStruct((2 * HALF, 2 * HALF, D), BF16),
            jax.ShapeDtypeStruct((D, D), F32),
        ),
        in_specs=[VMEM] * 5,
        out_specs=(VMEM, VMEM),
        compiler_params=PARAMS,
    )(g, own, lon, lat, diag)


def shifted(value, lat_step, lon_step):
    axes = (LAT if lat_step else ()) + (LON if lon_step else ())
    n_lat = lax.axis_size(LAT) if lat_step else 1
    n_lon = lax.axis_size(LON) if lon_step else 1
    pairs = []
    for a in range(n_lat):
        for b in range(n_lon):
            to = (a + lat_step) % n_lat * n_lon + (b + lon_step) % n_lon
            pairs.append((a * n_lon + b, to))
    return lax.ppermute(value, axes, pairs)


def per_device(tokens, cotangent, w_query, w_key, w_value, w_output):
    lat = shifted(jnp.stack([tokens[:HALF, HALF:], cotangent[:HALF, HALF:]]), -1, 0)
    lon = shifted(jnp.stack([tokens[HALF:, :HALF], cotangent[HALF:, :HALF]]), 0, -1)
    diag = shifted(jnp.stack([tokens[:HALF, :HALF], cotangent[:HALF, :HALF]]), -1, -1)
    last = (lax.axis_index(LAT) == lax.axis_size(LAT) - 1).astype(jnp.int32).reshape(1)
    wq, wk, wv, wo = load_weights(w_query, w_key, w_value, w_output)
    g, q, k, v, c = forward_call(last, tokens, cotangent, lon, lat, diag, wq, wk, wv)
    n_plane = lax.axis_size(PLANE)
    n_z = lax.axis_size("z")
    parts = g.reshape(n_plane, D // n_plane, D)
    parts = lax.all_to_all(parts, PLANE, 0, 0, tiled=True)
    own, lon, lat, diag = backward_call(last, q, k, v, c, wq, wk, wv, wo)
    parts = lax.all_to_all(sum_and_repeat(parts, n_z, own), "z", 0, 0, tiled=True)
    lat = shifted(lat, 1, 0)
    lon = shifted(lon, 0, 1)
    diag = shifted(diag, 1, 1)
    parts = sum_and_repeat(parts, n_plane // 2, lon, lat, diag)
    parts = lax.all_to_all(parts, ("y", "xh", "xl"), 0, 0, tiled=True)
    parts = lax.all_gather(parts.reshape(n_plane // 2, 1, D // n_plane, D), "core", axis=1, tiled=True)
    return finish_call(parts.reshape(D, D), own, lon, lat, diag)


def solution(mesh):
    fine = Mesh(mesh.devices.reshape(4, 2, 16, 2, 2), SPLIT)
    tiles = P(LAT, LON, None)
    return jax.shard_map(
        per_device,
        mesh=fine,
        in_specs=(tiles, tiles, P(), P(), P(), P()),
        out_specs=(tiles, P()),
        check_vma=False,
    )
```

```python
import math

import jax
import jax.numpy as jnp
from jax import lax
from jax.experimental import pallas as pl
from jax.experimental.pallas import tpu as pltpu
from jax.sharding import Mesh
from jax.sharding import PartitionSpec as P

HEADS = 16
DH = 32
D = 512
HALF = 6
FACTOR = 1.0 / math.sqrt(DH)
QUAD = HALF * HALF
N = 4 * QUAD
SPLIT = ("y", "xh", "zh", "zl", "xl", "core")
LAT = ("y", "xh")
LON = ("zh", "zl", "xl", "core")
CHIPS = ("y", "xh", "zl", "xl")
BLOCK = CHIPS + ("core",)
FAR_ORDER = [(4 + i) % 8 for i in range(8)]
CHIP_ORDER = [(22 + i) % 32 for i in range(32)]
BLOCK_ORDER = [2 * chip + core for chip in CHIP_ORDER for core in range(2)]
ROWS = 16
COLS = 512 // 2
F32 = jnp.float32
BF16 = jnp.bfloat16
NT = (((1,), (1,)), ((), ()))
VMEM = pl.BlockSpec(memory_space=pltpu.VMEM)
ANY = pl.BlockSpec(memory_space=pl.ANY)
HBM = pl.BlockSpec(memory_space=pltpu.HBM)
SMEM = pl.BlockSpec(memory_space=pltpu.SMEM)
MIB = 1024 * 1024
PARAMS = pltpu.CompilerParams(vmem_limit_bytes=12 * MIB)
WIDE = pltpu.CompilerParams(vmem_limit_bytes=52 * MIB)


def dot(a, b, dims=(((1,), (0,)), ((), ()))):
    return lax.dot_general(a, b, dims, preferred_element_type=F32)


def load_kernel(wq_ref, wk_ref, wv_ref, wo_ref, q_out, k_out, v_out, o_out, sems):
    pairs = ((wq_ref, q_out), (wk_ref, k_out), (wv_ref, v_out), (wo_ref, o_out))
    copies = [
        pltpu.make_async_copy(source, target, sems.at[i])
        for i, (source, target) in enumerate(pairs)
    ]
    for copy in copies:
        copy.start()
    for copy in copies:
        copy.wait()


def load_weights(*weights):
    return pl.pallas_call(
        load_kernel,
        out_shape=tuple(jax.ShapeDtypeStruct(w.shape, w.dtype) for w in weights),
        in_specs=[HBM] * 4,
        out_specs=(VMEM,) * 4,
        scratch_shapes=[pltpu.SemaphoreType.DMA((4,))],
        compiler_params=WIDE,
    )(*weights)


def score_bias(last):
    row = lax.broadcasted_iota(jnp.int32, (N, N), 0) >= 2 * QUAD
    col = lax.broadcasted_iota(jnp.int32, (N, N), 1) >= 2 * QUAD
    return jnp.where(jnp.logical_and(row != col, last == 1), F32(-1e30), F32(0.0))


def softmax_t(scores, bias):
    s = scores * (FACTOR * math.log2(math.e)) + bias
    e = jnp.exp2(s - jnp.max(s, axis=0, keepdims=True))
    return e * (1.0 / jnp.sum(e, axis=0, keepdims=True))


def staggered(depth, before, between, after):
    rows = [slice(DH * h, DH * (h + 1)) for h in range(HEADS)]
    ready = {h: before(rows[h]) for h in range(depth)}
    done = {}
    for h in range(HEADS + depth):
        if h + depth < HEADS:
            ready[h + depth] = before(rows[h + depth])
        if h >= depth:
            after(rows[h - depth], done.pop(h - depth))
        if h < HEADS:
            done[h] = between(ready.pop(h))


def forward_kernel(
    last_ref, tok_ref, cot_ref, lon_ref, lat_ref, diag_ref, wq_ref, wk_ref, wv_ref,
    g_ref, q_ref, k_ref, v_ref, c_ref,
    x_s, c_s, ot_s,
):
    for i in range(HALF):
        x_s[HALF * i : HALF * (i + 1), :] = tok_ref[HALF + i].astype(F32)[HALF:]
        c_s[HALF * i : HALF * (i + 1), :] = cot_ref[HALF + i].astype(F32)[HALF:]
        for part, ref in ((1, lon_ref), (2, lat_ref), (3, diag_ref)):
            at = QUAD * part + HALF * i
            x_s[at : at + HALF, :] = ref[0, i].astype(F32)
            c_s[at : at + HALF, :] = ref[1, i].astype(F32)
    x = x_s[...].astype(BF16)
    c = c_s[...].astype(BF16)
    q = dot(x, wq_ref[...]).astype(BF16)
    k = dot(x, wk_ref[...]).astype(BF16)
    v = dot(x, wv_ref[...]).astype(BF16)
    qt = q.T
    vt = v.T
    bias = score_bias(last_ref[0])

    def before(at):
        return dot(k[:, at], qt[at])

    def between(scores):
        return softmax_t(scores, bias).astype(BF16)

    def after(at, pb):
        ot_s[at, :] = dot(vt[at], pb).astype(BF16)

    staggered(3, before, between, after)
    g = dot(ot_s[...], c).astype(BF16).reshape(D // ROWS, ROWS, D)
    for j in range(D // COLS):
        g_ref[j] = g[:, :, COLS * j : COLS * (j + 1)]
    q_ref[...] = q
    k_ref[...] = k
    v_ref[...] = v
    c_ref[...] = c


def forward_call(last, tokens, cotangent, lon, lat, diag, wq, wk, wv):
    flat = jax.ShapeDtypeStruct((N, D), BF16)
    return pl.pallas_call(
        forward_kernel,
        out_shape=(jax.ShapeDtypeStruct((D // COLS, D // ROWS, ROWS, COLS), BF16), flat, flat, flat, flat),
        in_specs=[SMEM] + [VMEM] * 8,
        out_specs=(VMEM,) * 5,
        scratch_shapes=[
            pltpu.VMEM((N, D), F32),
            pltpu.VMEM((N, D), F32),
            pltpu.VMEM((D, N), BF16),
        ],
        compiler_params=PARAMS,
    )(last, tokens, cotangent, lon, lat, diag, wq, wk, wv)


def backward_kernel(
    last_ref, q_ref, k_ref, v_ref, c_ref, wq_ref, wk_ref, wv_ref, wo_ref,
    own_out, lat_out, side_out,
    dqt_s, dkt_s, dvt_s, dr_s,
):
    k = k_ref[...]
    v = v_ref[...]
    qt = q_ref[...].T
    kt = k.T
    dot_t = dot(wo_ref[...], c_ref[...], NT).astype(BF16)
    bias = score_bias(last_ref[0])

    def before(at):
        return dot(k[:, at], qt[at]), dot(v[:, at], dot_t[at])

    def between(products):
        scores, dp = products
        p = softmax_t(scores, bias)
        inner = jnp.sum(p * dp, axis=0, keepdims=True)
        return p.astype(BF16), (FACTOR * p * (dp - inner)).astype(BF16)

    def after(at, factors):
        pb, ds = factors
        dvt_s[at, :] = dot(dot_t[at], pb, NT).astype(BF16)
        dqt_s[at, :] = dot(kt[at], ds).astype(BF16)
        dkt_s[at, :] = dot(qt[at], ds, NT).astype(BF16)

    staggered(2, before, between, after)
    dr_s[...] = (
        dot(dqt_s[...].T, wq_ref[...], NT)
        + dot(dkt_s[...].T, wk_ref[...], NT)
        + dot(dvt_s[...].T, wv_ref[...], NT)
    )
    for part, ref in enumerate((own_out, side_out.at[0], lat_out, side_out.at[1])):
        for i in range(HALF):
            at = QUAD * part + HALF * i
            ref[i] = dr_s[at : at + HALF, :].astype(BF16)


def backward_call(last, q, k, v, c, wq, wk, wv, wo):
    quad = jax.ShapeDtypeStruct((HALF, HALF, D), BF16)
    return pl.pallas_call(
        backward_kernel,
        out_shape=(quad, quad, jax.ShapeDtypeStruct((2, HALF, HALF, D), BF16)),
        in_specs=[SMEM] + [VMEM] * 8,
        out_specs=(VMEM,) * 3,
        scratch_shapes=[
            pltpu.VMEM((D, N), BF16),
            pltpu.VMEM((D, N), BF16),
            pltpu.VMEM((D, N), BF16),
            pltpu.VMEM((N, D), F32),
        ],
        compiler_params=PARAMS,
    )(last, q, k, v, c, wq, wk, wv, wo)


def sum_and_join_kernel(in_ref, lat_ref, side_ref, out_ref, join_ref):
    join_ref[0] = lat_ref[...]
    join_ref[1] = side_ref[1]
    sum_kernel(in_ref, out_ref)


def sum_and_join(parts, copies, lat, side):
    return pl.pallas_call(
        sum_and_join_kernel,
        out_shape=(
            jax.ShapeDtypeStruct((copies,) + parts.shape[1:], BF16),
            jax.ShapeDtypeStruct(side.shape, BF16),
        ),
        in_specs=[VMEM] * 3,
        out_specs=(VMEM,) * 2,
        compiler_params=PARAMS,
    )(parts, lat, side)


def sum_kernel(in_ref, *rest):
    out_ref = rest[-1]
    total = in_ref[0].astype(F32)
    for i in range(1, in_ref.shape[0]):
        total = total + in_ref[i].astype(F32)
    total = total.astype(BF16)
    for i in range(out_ref.shape[0]):
        out_ref[i] = total


def sum_and_repeat(parts, copies, *after):
    return pl.pallas_call(
        sum_kernel,
        out_shape=jax.ShapeDtypeStruct((copies,) + parts.shape[1:], BF16),
        in_specs=[VMEM] + [ANY] * len(after),
        out_specs=VMEM,
        compiler_params=PARAMS,
    )(parts, *after)


def finish_kernel(g_ref, own_ref, side_ref, above_ref, dtok_ref, dout_ref):
    blocks = [g_ref[j].astype(F32).reshape(D, COLS) for j in range(D // COLS)]
    squares = sum(block * block for block in blocks)
    norm = jnp.sqrt(jnp.sum(squares, keepdims=True))
    scale = jnp.minimum(F32(1.0), F32(D) / (norm + 1e-6))
    for j, block in enumerate(blocks):
        dout_ref[:, COLS * j : COLS * (j + 1)] = block * scale
    for i in range(HALF):
        top = (above_ref[1, i].astype(F32), above_ref[0, i].astype(F32))
        dtok_ref[i] = jnp.concatenate(top, axis=0).astype(BF16)
        bottom = (side_ref[0, i].astype(F32), own_ref[i].astype(F32))
        dtok_ref[HALF + i] = jnp.concatenate(bottom, axis=0).astype(BF16)


def finish_call(g, own, side, above):
    return pl.pallas_call(
        finish_kernel,
        out_shape=(
            jax.ShapeDtypeStruct((2 * HALF, 2 * HALF, D), BF16),
            jax.ShapeDtypeStruct((D, D), F32),
        ),
        in_specs=[VMEM] * 4,
        out_specs=(VMEM, VMEM),
        compiler_params=PARAMS,
    )(g, own, side, above)


def shifted(value, lat_step, lon_step):
    axes = (LAT if lat_step else ()) + (LON if lon_step else ())
    n_lat = lax.axis_size(LAT) if lat_step else 1
    n_lon = lax.axis_size(LON) if lon_step else 1
    pairs = []
    for a in range(n_lat):
        for b in range(n_lon):
            to = (a + lat_step) % n_lat * n_lon + (b + lon_step) % n_lon
            pairs.append((a * n_lon + b, to))
    return lax.ppermute(value, axes, pairs)


def per_device(tokens, cotangent, w_query, w_key, w_value, w_output):
    lat = shifted(jnp.stack([tokens[:HALF, HALF:], cotangent[:HALF, HALF:]]), -1, 0)
    lon = shifted(jnp.stack([tokens[HALF:, :HALF], cotangent[HALF:, :HALF]]), 0, -1)
    diag = shifted(jnp.stack([tokens[:HALF, :HALF], cotangent[:HALF, :HALF]]), -1, -1)
    last = (lax.axis_index(LAT) == lax.axis_size(LAT) - 1).astype(jnp.int32).reshape(1)
    wq, wk, wv, wo = load_weights(w_query, w_key, w_value, w_output)
    g, q, k, v, c = forward_call(last, tokens, cotangent, lon, lat, diag, wq, wk, wv)
    n_chips = lax.axis_size(CHIPS)
    n_far = lax.axis_size("zh")
    parts = g.reshape(2 * n_chips, ROWS, COLS)
    parts = lax.all_to_all(parts, BLOCK, 0, 0, tiled=True)
    own, lat, side = backward_call(last, q, k, v, c, wq, wk, wv, wo)
    side = shifted(side, 0, 1)
    parts, above = sum_and_join(parts, n_far, lat, side)
    parts = lax.all_to_all(parts, "zh", 0, 0, axis_index_groups=[FAR_ORDER], tiled=True)
    above = shifted(above, 1, 0)
    parts = sum_and_repeat(parts, n_chips)
    parts = lax.all_to_all(parts, CHIPS, 0, 0, tiled=True)
    parts = parts.reshape(n_chips, 1, ROWS, COLS)
    parts = lax.all_gather(parts, "core", axis=1, tiled=True)
    parts = parts.reshape(D // COLS, D // ROWS, ROWS, COLS)
    return finish_call(parts, own, side, above)


def solution(mesh):
    fine = Mesh(mesh.devices.reshape(4, 2, 8, 2, 2, 2), SPLIT)
    tiles = P(LAT, LON, None)
    return jax.shard_map(
        per_device,
        mesh=fine,
        in_specs=(tiles, tiles, P(), P(), P(), P()),
        out_specs=(tiles, P()),
        check_vma=False,
    )
```

```python
import math

import jax
import jax.numpy as jnp
from jax import lax
from jax.experimental import pallas as pl
from jax.experimental.pallas import tpu as pltpu
from jax.sharding import Mesh
from jax.sharding import PartitionSpec as P

HEADS = 16
DH = 32
D = 512
HALF = 6
FACTOR = 1.0 / math.sqrt(DH)
QUAD = HALF * HALF
N = 4 * QUAD
SPLIT = ("y", "xh", "zh", "zl", "xl", "core")
LAT = ("y", "xh")
LON = ("zh", "zl", "xl", "core")
CHIPS = ("y", "xh", "zl", "xl")
BLOCK = CHIPS + ("core",)
FAR_ORDER = [(4 + i) % 8 for i in range(8)]
CHIP_ORDER = [(22 + i) % 32 for i in range(32)]
BLOCK_ORDER = [2 * chip + core for chip in CHIP_ORDER for core in range(2)]
ROWS = 16
COLS = 512 // 2
F32 = jnp.float32
BF16 = jnp.bfloat16
NT = (((1,), (1,)), ((), ()))
VMEM = pl.BlockSpec(memory_space=pltpu.VMEM)
ANY = pl.BlockSpec(memory_space=pl.ANY)
HBM = pl.BlockSpec(memory_space=pltpu.HBM)
SMEM = pl.BlockSpec(memory_space=pltpu.SMEM)
MIB = 1024 * 1024
PARAMS = pltpu.CompilerParams(vmem_limit_bytes=12 * MIB)
WIDE = pltpu.CompilerParams(vmem_limit_bytes=52 * MIB)


def dot(a, b, dims=(((1,), (0,)), ((), ()))):
    return lax.dot_general(a, b, dims, preferred_element_type=F32)


def load_kernel(wq_ref, wk_ref, wv_ref, wo_ref, q_out, k_out, v_out, o_out, sems):
    pairs = ((wq_ref, q_out), (wk_ref, k_out), (wv_ref, v_out), (wo_ref, o_out))
    copies = [
        pltpu.make_async_copy(source, target, sems.at[i])
        for i, (source, target) in enumerate(pairs)
    ]
    for copy in copies:
        copy.start()
    for copy in copies:
        copy.wait()


def load_weights(*weights):
    return pl.pallas_call(
        load_kernel,
        out_shape=tuple(jax.ShapeDtypeStruct(w.shape, w.dtype) for w in weights),
        in_specs=[HBM] * 4,
        out_specs=(VMEM,) * 4,
        scratch_shapes=[pltpu.SemaphoreType.DMA((4,))],
        compiler_params=WIDE,
    )(*weights)


def score_bias(last):
    row = lax.broadcasted_iota(jnp.int32, (N, N), 0) >= 2 * QUAD
    col = lax.broadcasted_iota(jnp.int32, (N, N), 1) >= 2 * QUAD
    return jnp.where(jnp.logical_and(row != col, last == 1), F32(-1e30), F32(0.0))


def softmax_t(scores, bias):
    s = scores * (FACTOR * math.log2(math.e)) + bias
    e = jnp.exp2(s - jnp.max(s, axis=0, keepdims=True))
    return e * (1.0 / jnp.sum(e, axis=0, keepdims=True))


def staggered(depth, before, between, after):
    rows = [slice(DH * h, DH * (h + 1)) for h in range(HEADS)]
    ready = {h: before(rows[h]) for h in range(depth)}
    done = {}
    for h in range(HEADS + depth):
        if h + depth < HEADS:
            ready[h + depth] = before(rows[h + depth])
        if h >= depth:
            after(rows[h - depth], done.pop(h - depth))
        if h < HEADS:
            done[h] = between(ready.pop(h))


def forward_kernel(
    last_ref, tok_ref, cot_ref, lon_ref, lat_ref, diag_ref, wq_ref, wk_ref, wv_ref,
    g_ref, q_ref, k_ref, v_ref, c_ref,
    x_s, c_s, ot_s,
):
    for i in range(HALF):
        x_s[HALF * i : HALF * (i + 1), :] = tok_ref[HALF + i].astype(F32)[HALF:]
        c_s[HALF * i : HALF * (i + 1), :] = cot_ref[HALF + i].astype(F32)[HALF:]
        for part, ref in ((1, lon_ref), (2, lat_ref), (3, diag_ref)):
            at = QUAD * part + HALF * i
            x_s[at : at + HALF, :] = ref[0, i].astype(F32)
            c_s[at : at + HALF, :] = ref[1, i].astype(F32)
    x = x_s[...].astype(BF16)
    c = c_s[...].astype(BF16)
    q = dot(x, wq_ref[...]).astype(BF16)
    k = dot(x, wk_ref[...]).astype(BF16)
    v = dot(x, wv_ref[...]).astype(BF16)
    qt = q.T
    vt = v.T
    bias = score_bias(last_ref[0])

    def before(at):
        return dot(k[:, at], qt[at])

    def between(scores):
        return softmax_t(scores, bias).astype(BF16)

    def after(at, pb):
        ot_s[at, :] = dot(vt[at], pb).astype(BF16)

    staggered(3, before, between, after)
    g = dot(ot_s[...], c).astype(BF16).reshape(D // ROWS, ROWS, D)
    for j in range(D // COLS):
        g_ref[j] = g[:, :, COLS * j : COLS * (j + 1)]
    q_ref[...] = q
    k_ref[...] = k
    v_ref[...] = v
    c_ref[...] = c


def forward_call(last, tokens, cotangent, lon, lat, diag, wq, wk, wv):
    flat = jax.ShapeDtypeStruct((N, D), BF16)
    return pl.pallas_call(
        forward_kernel,
        out_shape=(jax.ShapeDtypeStruct((D // COLS, D // ROWS, ROWS, COLS), BF16), flat, flat, flat, flat),
        in_specs=[SMEM] + [VMEM] * 8,
        out_specs=(VMEM,) * 5,
        scratch_shapes=[
            pltpu.VMEM((N, D), F32),
            pltpu.VMEM((N, D), F32),
            pltpu.VMEM((D, N), BF16),
        ],
        compiler_params=PARAMS,
    )(last, tokens, cotangent, lon, lat, diag, wq, wk, wv)


def backward_kernel(
    last_ref, q_ref, k_ref, v_ref, c_ref, wq_ref, wk_ref, wv_ref, wo_ref,
    own_out, lat_out, side_out,
    dqt_s, dkt_s, dvt_s, dr_s,
):
    k = k_ref[...]
    v = v_ref[...]
    qt = q_ref[...].T
    kt = k.T
    dot_t = dot(wo_ref[...], c_ref[...], NT).astype(BF16)
    bias = score_bias(last_ref[0])

    def before(at):
        return dot(k[:, at], qt[at]), dot(v[:, at], dot_t[at])

    def between(products):
        scores, dp = products
        p = softmax_t(scores, bias)
        inner = jnp.sum(p * dp, axis=0, keepdims=True)
        return p.astype(BF16), (FACTOR * p * (dp - inner)).astype(BF16)

    def after(at, factors):
        pb, ds = factors
        dvt_s[at, :] = dot(dot_t[at], pb, NT).astype(BF16)
        dqt_s[at, :] = dot(kt[at], ds).astype(BF16)
        dkt_s[at, :] = dot(qt[at], ds, NT).astype(BF16)

    staggered(2, before, between, after)
    dr_s[...] = (
        dot(dqt_s[...].T, wq_ref[...], NT)
        + dot(dkt_s[...].T, wk_ref[...], NT)
        + dot(dvt_s[...].T, wv_ref[...], NT)
    )
    for part, ref in enumerate((own_out, side_out.at[0], lat_out, side_out.at[1])):
        for i in range(HALF):
            at = QUAD * part + HALF * i
            ref[i] = dr_s[at : at + HALF, :].astype(BF16)


def backward_call(last, q, k, v, c, wq, wk, wv, wo):
    quad = jax.ShapeDtypeStruct((HALF, HALF, D), BF16)
    return pl.pallas_call(
        backward_kernel,
        out_shape=(quad, quad, jax.ShapeDtypeStruct((2, HALF, HALF, D), BF16)),
        in_specs=[SMEM] + [VMEM] * 8,
        out_specs=(VMEM,) * 3,
        scratch_shapes=[
            pltpu.VMEM((D, N), BF16),
            pltpu.VMEM((D, N), BF16),
            pltpu.VMEM((D, N), BF16),
            pltpu.VMEM((N, D), F32),
        ],
        compiler_params=PARAMS,
    )(last, q, k, v, c, wq, wk, wv, wo)


def sum_and_join_kernel(in_ref, lat_ref, side_ref, out_ref, join_ref):
    join_ref[0] = lat_ref[...]
    join_ref[1] = side_ref[1]
    sum_kernel(in_ref, out_ref)


def sum_and_join(parts, copies, lat, side):
    return pl.pallas_call(
        sum_and_join_kernel,
        out_shape=(
            jax.ShapeDtypeStruct((copies,) + parts.shape[1:], BF16),
            jax.ShapeDtypeStruct(side.shape, BF16),
        ),
        in_specs=[VMEM] * 3,
        out_specs=(VMEM,) * 2,
        compiler_params=PARAMS,
    )(parts, lat, side)


def sum_kernel(in_ref, *rest):
    out_ref = rest[-1]
    total = in_ref[0].astype(F32)
    for i in range(1, in_ref.shape[0]):
        total = total + in_ref[i].astype(F32)
    total = total.astype(BF16)
    for i in range(out_ref.shape[0]):
        out_ref[i] = total


def sum_and_repeat(parts, copies, *after):
    return pl.pallas_call(
        sum_kernel,
        out_shape=jax.ShapeDtypeStruct((copies,) + parts.shape[1:], BF16),
        in_specs=[VMEM] + [ANY] * len(after),
        out_specs=VMEM,
        compiler_params=PARAMS,
    )(parts, *after)


def finish_kernel(g_ref, own_ref, side_ref, above_ref, dtok_ref, dout_ref):
    rows = D // ROWS
    order = [(20 + p) % (2 * rows) for p in range(2 * rows)]
    blocks = [
        jnp.concatenate([g_ref[p].astype(F32) for p in order[rows * j : rows * (j + 1)]])
        for j in range(D // COLS)
    ]
    squares = sum(block * block for block in blocks)
    norm = jnp.sqrt(jnp.sum(squares, keepdims=True))
    scale = jnp.minimum(F32(1.0), F32(D) / (norm + 1e-6))
    for j, block in enumerate(blocks):
        dout_ref[:, COLS * j : COLS * (j + 1)] = block * scale
    for i in range(HALF):
        top = (above_ref[1, i].astype(F32), above_ref[0, i].astype(F32))
        dtok_ref[i] = jnp.concatenate(top, axis=0).astype(BF16)
        bottom = (side_ref[0, i].astype(F32), own_ref[i].astype(F32))
        dtok_ref[HALF + i] = jnp.concatenate(bottom, axis=0).astype(BF16)


def finish_call(g, own, side, above):
    return pl.pallas_call(
        finish_kernel,
        out_shape=(
            jax.ShapeDtypeStruct((2 * HALF, 2 * HALF, D), BF16),
            jax.ShapeDtypeStruct((D, D), F32),
        ),
        in_specs=[VMEM] * 4,
        out_specs=(VMEM, VMEM),
        compiler_params=PARAMS,
    )(g, own, side, above)


def shifted(value, lat_step, lon_step):
    axes = (LAT if lat_step else ()) + (LON if lon_step else ())
    n_lat = lax.axis_size(LAT) if lat_step else 1
    n_lon = lax.axis_size(LON) if lon_step else 1
    pairs = []
    for a in range(n_lat):
        for b in range(n_lon):
            to = (a + lat_step) % n_lat * n_lon + (b + lon_step) % n_lon
            pairs.append((a * n_lon + b, to))
    return lax.ppermute(value, axes, pairs)


def per_device(tokens, cotangent, w_query, w_key, w_value, w_output):
    lat = shifted(jnp.stack([tokens[:HALF, HALF:], cotangent[:HALF, HALF:]]), -1, 0)
    lon = shifted(jnp.stack([tokens[HALF:, :HALF], cotangent[HALF:, :HALF]]), 0, -1)
    diag = shifted(jnp.stack([tokens[:HALF, :HALF], cotangent[:HALF, :HALF]]), -1, -1)
    last = (lax.axis_index(LAT) == lax.axis_size(LAT) - 1).astype(jnp.int32).reshape(1)
    wq, wk, wv, wo = load_weights(w_query, w_key, w_value, w_output)
    g, q, k, v, c = forward_call(last, tokens, cotangent, lon, lat, diag, wq, wk, wv)
    n_chips = lax.axis_size(CHIPS)
    n_far = lax.axis_size("zh")
    parts = g.reshape(2 * n_chips, ROWS, COLS)
    parts = lax.all_to_all(parts, BLOCK, 0, 0, tiled=True)
    own, lat, side = backward_call(last, q, k, v, c, wq, wk, wv, wo)
    side = shifted(side, 0, 1)
    parts, above = sum_and_join(parts, n_far, lat, side)
    parts = lax.all_to_all(parts, "zh", 0, 0, axis_index_groups=[FAR_ORDER], tiled=True)
    above = shifted(above, 1, 0)
    parts = sum_and_repeat(parts, n_chips)
    parts = lax.all_to_all(parts, CHIPS, 0, 0, axis_index_groups=[CHIP_ORDER], tiled=True)
    parts = parts.reshape(n_chips, 1, ROWS, COLS)
    parts = lax.all_gather(parts, "core", axis=1, tiled=True)
    parts = parts.reshape(2 * n_chips, ROWS, COLS)
    return finish_call(parts, own, side, above)


def solution(mesh):
    fine = Mesh(mesh.devices.reshape(4, 2, 8, 2, 2, 2), SPLIT)
    tiles = P(LAT, LON, None)
    return jax.shard_map(
        per_device,
        mesh=fine,
        in_specs=(tiles, tiles, P(), P(), P(), P()),
        out_specs=(tiles, P()),
        check_vma=False,
    )
```

```python
import math

import jax
import jax.numpy as jnp
from jax import lax
from jax.experimental import pallas as pl
from jax.experimental.pallas import tpu as pltpu
from jax.sharding import Mesh
from jax.sharding import PartitionSpec as P

HEADS = 16
DH = 32
D = 512
HALF = 6
FACTOR = 1.0 / math.sqrt(DH)
QUAD = HALF * HALF
N = 4 * QUAD
SPLIT = ("y", "xh", "zh", "zl", "xl", "core")
LAT = ("y", "xh")
LON = ("zh", "zl", "xl", "core")
CHIPS = ("y", "xh", "zl", "xl")
BLOCK = CHIPS + ("core",)
FAR_ORDER = [(4 + i) % 8 for i in range(8)]
CHIP_ORDER = [(22 + i) % 32 for i in range(32)]
BLOCK_ORDER = [2 * chip + core for chip in CHIP_ORDER for core in range(2)]
ROWS = 16
COLS = 512 // 2
F32 = jnp.float32
BF16 = jnp.bfloat16
NT = (((1,), (1,)), ((), ()))
VMEM = pl.BlockSpec(memory_space=pltpu.VMEM)
ANY = pl.BlockSpec(memory_space=pl.ANY)
HBM = pl.BlockSpec(memory_space=pltpu.HBM)
SMEM = pl.BlockSpec(memory_space=pltpu.SMEM)
MIB = 1024 * 1024
PARAMS = pltpu.CompilerParams(vmem_limit_bytes=12 * MIB)
WIDE = pltpu.CompilerParams(vmem_limit_bytes=52 * MIB)


def dot(a, b, dims=(((1,), (0,)), ((), ()))):
    return lax.dot_general(a, b, dims, preferred_element_type=F32)


def load_kernel(wq_ref, wk_ref, wv_ref, wo_ref, q_out, k_out, v_out, o_out, sems):
    pairs = ((wq_ref, q_out), (wk_ref, k_out), (wv_ref, v_out), (wo_ref, o_out))
    copies = [
        pltpu.make_async_copy(source, target, sems.at[i])
        for i, (source, target) in enumerate(pairs)
    ]
    for copy in copies:
        copy.start()
    for copy in copies:
        copy.wait()


def load_weights(*weights):
    return pl.pallas_call(
        load_kernel,
        out_shape=tuple(jax.ShapeDtypeStruct(w.shape, w.dtype) for w in weights),
        in_specs=[HBM] * 4,
        out_specs=(VMEM,) * 4,
        scratch_shapes=[pltpu.SemaphoreType.DMA((4,))],
        compiler_params=WIDE,
    )(*weights)


def score_bias(last):
    row = lax.broadcasted_iota(jnp.int32, (N, N), 0) >= 2 * QUAD
    col = lax.broadcasted_iota(jnp.int32, (N, N), 1) >= 2 * QUAD
    return jnp.where(jnp.logical_and(row != col, last == 1), F32(-1e30), F32(0.0))


def softmax_t(scores, bias):
    s = scores * (FACTOR * math.log2(math.e)) + bias
    e = jnp.exp2(s - jnp.max(s, axis=0, keepdims=True))
    return e * (1.0 / jnp.sum(e, axis=0, keepdims=True))


def staggered(depth, before, between, after):
    rows = [slice(DH * h, DH * (h + 1)) for h in range(HEADS)]
    ready = {h: before(rows[h]) for h in range(depth)}
    done = {}
    for h in range(HEADS + depth):
        if h + depth < HEADS:
            ready[h + depth] = before(rows[h + depth])
        if h >= depth:
            after(rows[h - depth], done.pop(h - depth))
        if h < HEADS:
            done[h] = between(ready.pop(h))


def forward_kernel(
    last_ref, tok_ref, cot_ref, diag_ref, lat_ref, lon_ref, wq_ref, wk_ref, wv_ref,
    g_ref, q_ref, k_ref, v_ref, c_ref,
    x_s, c_s, ot_s,
):
    for i in range(HALF):
        x_s[HALF * i : HALF * (i + 1), :] = tok_ref[HALF + i].astype(F32)[HALF:]
        c_s[HALF * i : HALF * (i + 1), :] = cot_ref[HALF + i].astype(F32)[HALF:]
        for part, ref in ((1, lon_ref), (2, lat_ref), (3, diag_ref)):
            at = QUAD * part + HALF * i
            x_s[at : at + HALF, :] = ref[0, i].astype(F32)
            c_s[at : at + HALF, :] = ref[1, i].astype(F32)
    x = x_s[...].astype(BF16)
    c = c_s[...].astype(BF16)
    q = dot(x, wq_ref[...]).astype(BF16)
    k = dot(x, wk_ref[...]).astype(BF16)
    v = dot(x, wv_ref[...]).astype(BF16)
    qt = q.T
    vt = v.T
    bias = score_bias(last_ref[0])

    def before(at):
        return dot(k[:, at], qt[at])

    def between(scores):
        return softmax_t(scores, bias).astype(BF16)

    def after(at, pb):
        ot_s[at, :] = dot(vt[at], pb).astype(BF16)

    staggered(3, before, between, after)
    g = dot(ot_s[...], c).astype(BF16).reshape(D // ROWS, ROWS, D)
    for j in range(D // COLS):
        g_ref[j] = g[:, :, COLS * j : COLS * (j + 1)]
    q_ref[...] = q
    k_ref[...] = k
    v_ref[...] = v
    c_ref[...] = c


def forward_call(last, tokens, cotangent, diag, lat, lon, wq, wk, wv):
    flat = jax.ShapeDtypeStruct((N, D), BF16)
    return pl.pallas_call(
        forward_kernel,
        out_shape=(jax.ShapeDtypeStruct((D // COLS, D // ROWS, ROWS, COLS), BF16), flat, flat, flat, flat),
        in_specs=[SMEM] + [VMEM] * 8,
        out_specs=(VMEM,) * 5,
        scratch_shapes=[
            pltpu.VMEM((N, D), F32),
            pltpu.VMEM((N, D), F32),
            pltpu.VMEM((D, N), BF16),
        ],
        compiler_params=PARAMS,
    )(last, tokens, cotangent, diag, lat, lon, wq, wk, wv)


def backward_kernel(
    last_ref, q_ref, k_ref, v_ref, c_ref, wq_ref, wk_ref, wv_ref, wo_ref,
    own_out, lat_out, side_out,
    dqt_s, dkt_s, dvt_s, dr_s,
):
    k = k_ref[...]
    v = v_ref[...]
    qt = q_ref[...].T
    kt = k.T
    dot_t = dot(wo_ref[...], c_ref[...], NT).astype(BF16)
    bias = score_bias(last_ref[0])

    def before(at):
        return dot(k[:, at], qt[at]), dot(v[:, at], dot_t[at])

    def between(products):
        scores, dp = products
        p = softmax_t(scores, bias)
        inner = jnp.sum(p * dp, axis=0, keepdims=True)
        return p.astype(BF16), (FACTOR * p * (dp - inner)).astype(BF16)

    def after(at, factors):
        pb, ds = factors
        dvt_s[at, :] = dot(dot_t[at], pb, NT).astype(BF16)
        dqt_s[at, :] = dot(kt[at], ds).astype(BF16)
        dkt_s[at, :] = dot(qt[at], ds, NT).astype(BF16)

    staggered(2, before, between, after)
    dr_s[...] = (
        dot(dqt_s[...].T, wq_ref[...], NT)
        + dot(dkt_s[...].T, wk_ref[...], NT)
        + dot(dvt_s[...].T, wv_ref[...], NT)
    )
    for part, ref in enumerate((own_out, side_out.at[0], lat_out, side_out.at[1])):
        for i in range(HALF):
            at = QUAD * part + HALF * i
            ref[i] = dr_s[at : at + HALF, :].astype(BF16)


def backward_call(last, q, k, v, c, wq, wk, wv, wo):
    quad = jax.ShapeDtypeStruct((HALF, HALF, D), BF16)
    return pl.pallas_call(
        backward_kernel,
        out_shape=(quad, quad, jax.ShapeDtypeStruct((2, HALF, HALF, D), BF16)),
        in_specs=[SMEM] + [VMEM] * 8,
        out_specs=(VMEM,) * 3,
        scratch_shapes=[
            pltpu.VMEM((D, N), BF16),
            pltpu.VMEM((D, N), BF16),
            pltpu.VMEM((D, N), BF16),
            pltpu.VMEM((N, D), F32),
        ],
        compiler_params=PARAMS,
    )(last, q, k, v, c, wq, wk, wv, wo)


def sum_and_join_kernel(in_ref, lat_ref, side_ref, out_ref, join_ref):
    join_ref[0] = lat_ref[...]
    join_ref[1] = side_ref[1]
    sum_kernel(in_ref, out_ref)


def sum_and_join(parts, copies, lat, side):
    return pl.pallas_call(
        sum_and_join_kernel,
        out_shape=(
            jax.ShapeDtypeStruct((copies,) + parts.shape[1:], BF16),
            jax.ShapeDtypeStruct(side.shape, BF16),
        ),
        in_specs=[VMEM] * 3,
        out_specs=(VMEM,) * 2,
        compiler_params=PARAMS,
    )(parts, lat, side)


def sum_kernel(in_ref, *rest):
    out_ref = rest[-1]
    total = in_ref[0].astype(F32)
    for i in range(1, in_ref.shape[0]):
        total = total + in_ref[i].astype(F32)
    total = total.astype(BF16)
    for i in range(out_ref.shape[0]):
        out_ref[i] = total


def sum_and_repeat(parts, copies, *after):
    return pl.pallas_call(
        sum_kernel,
        out_shape=jax.ShapeDtypeStruct((copies,) + parts.shape[1:], BF16),
        in_specs=[VMEM] + [ANY] * len(after),
        out_specs=VMEM,
        compiler_params=PARAMS,
    )(parts, *after)


def finish_kernel(g_ref, own_ref, side_ref, above_ref, dtok_ref, dout_ref):
    rows = D // ROWS
    order = [(20 + p) % (2 * rows) for p in range(2 * rows)]
    blocks = [
        jnp.concatenate([g_ref[p].astype(F32) for p in order[rows * j : rows * (j + 1)]])
        for j in range(D // COLS)
    ]
    squares = sum(block * block for block in blocks)
    norm = jnp.sqrt(jnp.sum(squares, keepdims=True))
    scale = jnp.minimum(F32(1.0), F32(D) / (norm + 1e-6))
    for j, block in enumerate(blocks):
        dout_ref[:, COLS * j : COLS * (j + 1)] = block * scale
    for i in range(HALF):
        top = (above_ref[1, i].astype(F32), above_ref[0, i].astype(F32))
        dtok_ref[i] = jnp.concatenate(top, axis=0).astype(BF16)
        bottom = (side_ref[0, i].astype(F32), own_ref[i].astype(F32))
        dtok_ref[HALF + i] = jnp.concatenate(bottom, axis=0).astype(BF16)


def finish_call(g, own, side, above):
    return pl.pallas_call(
        finish_kernel,
        out_shape=(
            jax.ShapeDtypeStruct((2 * HALF, 2 * HALF, D), BF16),
            jax.ShapeDtypeStruct((D, D), F32),
        ),
        in_specs=[VMEM] * 4,
        out_specs=(VMEM, VMEM),
        compiler_params=PARAMS,
    )(g, own, side, above)


def shifted(value, lat_step, lon_step):
    axes = (LAT if lat_step else ()) + (LON if lon_step else ())
    n_lat = lax.axis_size(LAT) if lat_step else 1
    n_lon = lax.axis_size(LON) if lon_step else 1
    pairs = []
    for a in range(n_lat):
        for b in range(n_lon):
            to = (a + lat_step) % n_lat * n_lon + (b + lon_step) % n_lon
            pairs.append((a * n_lon + b, to))
    return lax.ppermute(value, axes, pairs)


def per_device(tokens, cotangent, w_query, w_key, w_value, w_output):
    diag = shifted(jnp.stack([tokens[:HALF, :HALF], cotangent[:HALF, :HALF]]), -1, -1)
    lat = shifted(jnp.stack([tokens[:HALF, HALF:], cotangent[:HALF, HALF:]]), -1, 0)
    lon = shifted(jnp.stack([tokens[HALF:, :HALF], cotangent[HALF:, :HALF]]), 0, -1)
    last = (lax.axis_index(LAT) == lax.axis_size(LAT) - 1).astype(jnp.int32).reshape(1)
    wq, wk, wv, wo = load_weights(w_query, w_key, w_value, w_output)
    g, q, k, v, c = forward_call(last, tokens, cotangent, diag, lat, lon, wq, wk, wv)
    n_chips = lax.axis_size(CHIPS)
    n_far = lax.axis_size("zh")
    parts = g.reshape(2 * n_chips, ROWS, COLS)
    parts = lax.all_to_all(parts, BLOCK, 0, 0, tiled=True)
    own, lat, side = backward_call(last, q, k, v, c, wq, wk, wv, wo)
    side = shifted(side, 0, 1)
    parts, above = sum_and_join(parts, n_far, lat, side)
    parts = lax.all_to_all(parts, "zh", 0, 0, axis_index_groups=[FAR_ORDER], tiled=True)
    above = shifted(above, 1, 0)
    parts = sum_and_repeat(parts, n_chips)
    parts = lax.all_to_all(parts, CHIPS, 0, 0, axis_index_groups=[CHIP_ORDER], tiled=True)
    parts = parts.reshape(n_chips, 1, ROWS, COLS)
    parts = lax.all_gather(parts, "core", axis=1, tiled=True)
    parts = parts.reshape(2 * n_chips, ROWS, COLS)
    return finish_call(parts, own, side, above)


def solution(mesh):
    fine = Mesh(mesh.devices.reshape(4, 2, 8, 2, 2, 2), SPLIT)
    tiles = P(LAT, LON, None)
    return jax.shard_map(
        per_device,
        mesh=fine,
        in_specs=(tiles, tiles, P(), P(), P(), P()),
        out_specs=(tiles, P()),
        check_vma=False,
    )
```

```python
import math

import jax
import jax.numpy as jnp
from jax import lax
from jax.experimental import pallas as pl
from jax.experimental.pallas import tpu as pltpu
from jax.sharding import Mesh
from jax.sharding import PartitionSpec as P

HEADS = 16
DH = 32
D = 512
HALF = 6
FACTOR = 1.0 / math.sqrt(DH)
QUAD = HALF * HALF
N = 4 * QUAD
SPLIT = ("y", "xh", "zh", "zl", "xl", "core")
LAT = ("y", "xh")
LON = ("zh", "zl", "xl", "core")
CHIPS = ("y", "xh", "zl", "xl")
BLOCK = CHIPS + ("core",)
FAR_ORDER = [(4 + i) % 8 for i in range(8)]
CHIP_ORDER = [(22 + i) % 32 for i in range(32)]
BLOCK_ORDER = [2 * chip + core for chip in CHIP_ORDER for core in range(2)]
ROWS = 16
COLS = 512 // 2
F32 = jnp.float32
BF16 = jnp.bfloat16
NT = (((1,), (1,)), ((), ()))
VMEM = pl.BlockSpec(memory_space=pltpu.VMEM)
ANY = pl.BlockSpec(memory_space=pl.ANY)
HBM = pl.BlockSpec(memory_space=pltpu.HBM)
SMEM = pl.BlockSpec(memory_space=pltpu.SMEM)
MIB = 1024 * 1024
PARAMS = pltpu.CompilerParams(vmem_limit_bytes=12 * MIB)
WIDE = pltpu.CompilerParams(vmem_limit_bytes=52 * MIB)


def dot(a, b, dims=(((1,), (0,)), ((), ()))):
    return lax.dot_general(a, b, dims, preferred_element_type=F32)


def load_kernel(wq_ref, wk_ref, wv_ref, q_out, k_out, v_out, sems):
    pairs = ((wq_ref, q_out), (wk_ref, k_out), (wv_ref, v_out))
    copies = [
        pltpu.make_async_copy(source, target, sems.at[i])
        for i, (source, target) in enumerate(pairs)
    ]
    for copy in copies:
        copy.start()
    for copy in copies:
        copy.wait()


def load_weights(*weights):
    return pl.pallas_call(
        load_kernel,
        out_shape=tuple(jax.ShapeDtypeStruct(w.shape, w.dtype) for w in weights),
        in_specs=[HBM] * 3,
        out_specs=(VMEM,) * 3,
        scratch_shapes=[pltpu.SemaphoreType.DMA((3,))],
        compiler_params=WIDE,
    )(*weights)


def score_bias(last):
    row = lax.broadcasted_iota(jnp.int32, (N, N), 0) >= 2 * QUAD
    col = lax.broadcasted_iota(jnp.int32, (N, N), 1) >= 2 * QUAD
    return jnp.where(jnp.logical_and(row != col, last == 1), F32(-1e30), F32(0.0))


def softmax_t(scores, bias):
    s = scores * (FACTOR * math.log2(math.e)) + bias
    e = jnp.exp2(s - jnp.max(s, axis=0, keepdims=True))
    return e * (1.0 / jnp.sum(e, axis=0, keepdims=True))


def staggered(depth, before, between, after):
    rows = [slice(DH * h, DH * (h + 1)) for h in range(HEADS)]
    ready = {h: before(rows[h]) for h in range(depth)}
    done = {}
    for h in range(HEADS + depth):
        if h + depth < HEADS:
            ready[h + depth] = before(rows[h + depth])
        if h >= depth:
            after(rows[h - depth], done.pop(h - depth))
        if h < HEADS:
            done[h] = between(ready.pop(h))


def forward_kernel(
    last_ref, tok_ref, cot_ref, diag_ref, lat_ref, lon_ref, wq_ref, wk_ref, wv_ref,
    g_ref, q_ref, k_ref, v_ref, c_ref,
    x_s, c_s, ot_s,
):
    for i in range(HALF):
        x_s[HALF * i : HALF * (i + 1), :] = tok_ref[HALF + i].astype(F32)[HALF:]
        c_s[HALF * i : HALF * (i + 1), :] = cot_ref[HALF + i].astype(F32)[HALF:]
        for part, ref in ((1, lon_ref), (2, lat_ref), (3, diag_ref)):
            at = QUAD * part + HALF * i
            x_s[at : at + HALF, :] = ref[0, i].astype(F32)
            c_s[at : at + HALF, :] = ref[1, i].astype(F32)
    x = x_s[...].astype(BF16)
    c = c_s[...].astype(BF16)
    q = dot(x, wq_ref[...]).astype(BF16)
    k = dot(x, wk_ref[...]).astype(BF16)
    v = dot(x, wv_ref[...]).astype(BF16)
    qt = q.T
    vt = v.T
    bias = score_bias(last_ref[0])

    def before(at):
        return dot(k[:, at], qt[at])

    def between(scores):
        return softmax_t(scores, bias).astype(BF16)

    def after(at, pb):
        ot_s[at, :] = dot(vt[at], pb).astype(BF16)

    staggered(3, before, between, after)
    g = dot(ot_s[...], c).astype(BF16).reshape(D // ROWS, ROWS, D)
    for j in range(D // COLS):
        g_ref[j] = g[:, :, COLS * j : COLS * (j + 1)]
    q_ref[...] = q
    k_ref[...] = k
    v_ref[...] = v
    c_ref[...] = c


def forward_call(last, tokens, cotangent, diag, lat, lon, wq, wk, wv):
    flat = jax.ShapeDtypeStruct((N, D), BF16)
    return pl.pallas_call(
        forward_kernel,
        out_shape=(jax.ShapeDtypeStruct((D // COLS, D // ROWS, ROWS, COLS), BF16), flat, flat, flat, flat),
        in_specs=[SMEM] + [VMEM] * 8,
        out_specs=(VMEM,) * 5,
        scratch_shapes=[
            pltpu.VMEM((N, D), F32),
            pltpu.VMEM((N, D), F32),
            pltpu.VMEM((D, N), BF16),
        ],
        compiler_params=PARAMS,
    )(last, tokens, cotangent, diag, lat, lon, wq, wk, wv)


def backward_kernel(
    last_ref, q_ref, k_ref, v_ref, c_ref, wq_ref, wk_ref, wv_ref, wo_ref,
    own_out, lat_out, side_out,
    dqt_s, dkt_s, dvt_s, dr_s,
):
    k = k_ref[...]
    v = v_ref[...]
    qt = q_ref[...].T
    kt = k.T
    dot_t = dot(wo_ref[...], c_ref[...], NT).astype(BF16)
    bias = score_bias(last_ref[0])

    def before(at):
        return dot(k[:, at], qt[at]), dot(v[:, at], dot_t[at])

    def between(products):
        scores, dp = products
        p = softmax_t(scores, bias)
        inner = jnp.sum(p * dp, axis=0, keepdims=True)
        return p.astype(BF16), (FACTOR * p * (dp - inner)).astype(BF16)

    def after(at, factors):
        pb, ds = factors
        dvt_s[at, :] = dot(dot_t[at], pb, NT).astype(BF16)
        dqt_s[at, :] = dot(kt[at], ds).astype(BF16)
        dkt_s[at, :] = dot(qt[at], ds, NT).astype(BF16)

    staggered(2, before, between, after)
    dr_s[...] = (
        dot(dqt_s[...].T, wq_ref[...], NT)
        + dot(dkt_s[...].T, wk_ref[...], NT)
        + dot(dvt_s[...].T, wv_ref[...], NT)
    )
    for part, ref in enumerate((own_out, side_out.at[0], lat_out, side_out.at[1])):
        for i in range(HALF):
            at = QUAD * part + HALF * i
            ref[i] = dr_s[at : at + HALF, :].astype(BF16)


def backward_call(last, q, k, v, c, wq, wk, wv, wo):
    quad = jax.ShapeDtypeStruct((HALF, HALF, D), BF16)
    return pl.pallas_call(
        backward_kernel,
        out_shape=(quad, quad, jax.ShapeDtypeStruct((2, HALF, HALF, D), BF16)),
        in_specs=[SMEM] + [VMEM] * 8,
        out_specs=(VMEM,) * 3,
        scratch_shapes=[
            pltpu.VMEM((D, N), BF16),
            pltpu.VMEM((D, N), BF16),
            pltpu.VMEM((D, N), BF16),
            pltpu.VMEM((N, D), F32),
        ],
        compiler_params=PARAMS,
    )(last, q, k, v, c, wq, wk, wv, wo)


def sum_and_join_kernel(in_ref, lat_ref, side_ref, out_ref, join_ref):
    join_ref[0] = lat_ref[...]
    join_ref[1] = side_ref[1]
    sum_kernel(in_ref, out_ref)


def sum_and_join(parts, copies, lat, side):
    return pl.pallas_call(
        sum_and_join_kernel,
        out_shape=(
            jax.ShapeDtypeStruct((copies,) + parts.shape[1:], BF16),
            jax.ShapeDtypeStruct(side.shape, BF16),
        ),
        in_specs=[VMEM] * 3,
        out_specs=(VMEM,) * 2,
        compiler_params=PARAMS,
    )(parts, lat, side)


def sum_kernel(in_ref, *rest):
    out_ref = rest[-1]
    total = in_ref[0].astype(F32)
    for i in range(1, in_ref.shape[0]):
        total = total + in_ref[i].astype(F32)
    total = total.astype(BF16)
    for i in range(out_ref.shape[0]):
        out_ref[i] = total


def sum_and_repeat(parts, copies, *after):
    return pl.pallas_call(
        sum_kernel,
        out_shape=jax.ShapeDtypeStruct((copies,) + parts.shape[1:], BF16),
        in_specs=[VMEM] + [ANY] * len(after),
        out_specs=VMEM,
        compiler_params=PARAMS,
    )(parts, *after)


def finish_kernel(g_ref, own_ref, side_ref, above_ref, dtok_ref, dout_ref):
    rows = D // ROWS
    order = [(20 + p) % (2 * rows) for p in range(2 * rows)]
    blocks = [
        jnp.concatenate([g_ref[p].astype(F32) for p in order[rows * j : rows * (j + 1)]])
        for j in range(D // COLS)
    ]
    squares = sum(block * block for block in blocks)
    norm = jnp.sqrt(jnp.sum(squares, keepdims=True))
    scale = jnp.minimum(F32(1.0), F32(D) / (norm + 1e-6))
    for j, block in enumerate(blocks):
        dout_ref[:, COLS * j : COLS * (j + 1)] = block * scale
    for i in range(HALF):
        top = (above_ref[1, i].astype(F32), above_ref[0, i].astype(F32))
        dtok_ref[i] = jnp.concatenate(top, axis=0).astype(BF16)
        bottom = (side_ref[0, i].astype(F32), own_ref[i].astype(F32))
        dtok_ref[HALF + i] = jnp.concatenate(bottom, axis=0).astype(BF16)


def finish_call(g, own, side, above):
    return pl.pallas_call(
        finish_kernel,
        out_shape=(
            jax.ShapeDtypeStruct((2 * HALF, 2 * HALF, D), BF16),
            jax.ShapeDtypeStruct((D, D), F32),
        ),
        in_specs=[VMEM] * 4,
        out_specs=(VMEM, VMEM),
        compiler_params=PARAMS,
    )(g, own, side, above)


def shifted(value, lat_step, lon_step):
    axes = (LAT if lat_step else ()) + (LON if lon_step else ())
    n_lat = lax.axis_size(LAT) if lat_step else 1
    n_lon = lax.axis_size(LON) if lon_step else 1
    pairs = []
    for a in range(n_lat):
        for b in range(n_lon):
            to = (a + lat_step) % n_lat * n_lon + (b + lon_step) % n_lon
            pairs.append((a * n_lon + b, to))
    return lax.ppermute(value, axes, pairs)


def per_device(tokens, cotangent, w_query, w_key, w_value, w_output):
    diag = shifted(jnp.stack([tokens[:HALF, :HALF], cotangent[:HALF, :HALF]]), -1, -1)
    lat = shifted(jnp.stack([tokens[:HALF, HALF:], cotangent[:HALF, HALF:]]), -1, 0)
    lon = shifted(jnp.stack([tokens[HALF:, :HALF], cotangent[HALF:, :HALF]]), 0, -1)
    last = (lax.axis_index(LAT) == lax.axis_size(LAT) - 1).astype(jnp.int32).reshape(1)
    wq, wk, wv = load_weights(w_query, w_key, w_value)
    g, q, k, v, c = forward_call(last, tokens, cotangent, diag, lat, lon, wq, wk, wv)
    n_chips = lax.axis_size(CHIPS)
    n_far = lax.axis_size("zh")
    parts = g.reshape(2 * n_chips, ROWS, COLS)
    parts = lax.all_to_all(parts, BLOCK, 0, 0, tiled=True)
    own, lat, side = backward_call(last, q, k, v, c, wq, wk, wv, w_output)
    side = shifted(side, 0, 1)
    parts, above = sum_and_join(parts, n_far, lat, side)
    parts = lax.all_to_all(parts, "zh", 0, 0, axis_index_groups=[FAR_ORDER], tiled=True)
    above = shifted(above, 1, 0)
    parts = sum_and_repeat(parts, n_chips)
    parts = lax.all_to_all(parts, CHIPS, 0, 0, axis_index_groups=[CHIP_ORDER], tiled=True)
    parts = parts.reshape(n_chips, 1, ROWS, COLS)
    parts = lax.all_gather(parts, "core", axis=1, tiled=True)
    parts = parts.reshape(2 * n_chips, ROWS, COLS)
    return finish_call(parts, own, side, above)


def solution(mesh):
    fine = Mesh(mesh.devices.reshape(4, 2, 8, 2, 2, 2), SPLIT)
    tiles = P(LAT, LON, None)
    return jax.shard_map(
        per_device,
        mesh=fine,
        in_specs=(tiles, tiles, P(), P(), P(), P()),
        out_specs=(tiles, P()),
        check_vma=False,
    )
```
